32 devices in a mesh: dp: 2 (over x), seq: 8 (over z, core), tensor: 2 (over y).
Axes of the slice: x: 2, y: 2, z: 4, core: 2. Of those that a mesh axis runs over, the one named last changes fastest.
Arguments:
- queries: bfloat16 [2, 2048, 2048], P('dp', 'seq', 'tensor'), may hold values from -100 to 100
- image_keys: bfloat16 [2, 256, 256], P('dp', 'seq', 'tensor'), may hold values from -9 to 9
- image_states: bfloat16 [2, 256, 8192], P('dp', 'seq'), may hold values from -6 to 6
- value_weight: bfloat16 [8192, 256], P('seq', 'tensor'), may hold values from -0.0625 to 0.0625
- out_grad: bfloat16 [2, 2048, 2048], P('dp', 'seq', 'tensor'), may hold values from -6 to 6
Outputs:
- query_grad: bfloat16 [2, 2048, 2048], P('dp', 'seq', 'tensor')
- key_grad: bfloat16 [2, 256, 256], P('dp', 'seq', 'tensor')
- weight_grad: bfloat16 [8192, 256], P('seq', 'tensor')
- image_grad: bfloat16 [2, 256, 8192], P('dp', 'seq', 'tensor')
The draws below stay inside these ranges and needn't reach their ends.
All inputs are finite; a program needn't handle non-finite values.
Results may differ from the reference program's by a relative error of at most 0.02.
Values may be sent and summed in bfloat16 or wider, within the bound.
A program may use at most 64 MiB of HBM per device.

```python
import math
import jax
import jax.numpy as jnp
from jax import lax

D = 8192
HD = 128
GROUP = 8
KV_DEV = 1
IMG_DEV = 32
KV_HEADS = 2
HEADS = 16
TEXT = 2048
IMG = 256
N_DP = 2
N_SEQ = 8
N_TENSOR = 2


def shared_keys(rng_key):
    base_draw = jax.random.truncated_normal(jax.random.fold_in(rng_key, 11), -4.0, 4.0, (N_DP, IMG, KV_HEADS, HD), jnp.float32)
    spread = jnp.exp(jax.random.uniform(jax.random.fold_in(rng_key, 12), (N_DP, IMG, 1, 1), jnp.float32, math.log(0.5), math.log(2.0)))
    return base_draw * spread


def draw_image_keys(key, part):
    key_draw = shared_keys(key)
    return key_draw.reshape(N_DP, IMG, KV_HEADS * HD).astype(jnp.bfloat16)


def draw_queries(key, part):
    key = jax.random.fold_in(key, 2)
    full_shape = (N_DP, TEXT, KV_HEADS, GROUP, HD)
    spread = jnp.exp(jax.random.uniform(jax.random.fold_in(key, 21), (N_DP, TEXT, 1, 1, 1), jnp.float32, math.log(0.5), math.log(2.0)))
    values = jax.random.truncated_normal(jax.random.fold_in(key, 22), -4.0, 4.0, full_shape, jnp.float32) * spread
    return values.reshape(N_DP, TEXT, KV_HEADS * GROUP * HD).astype(jnp.bfloat16)


def steps_of(own_key, extent, split, smallest, top_value):
    def one(dim, shards_of):
        heights = jax.random.uniform(jax.random.fold_in(jax.random.fold_in(own_key, 6), dim), (shards_of,), jnp.float32, smallest / len(split), top_value / len(split))
        return jnp.repeat(jnp.exp(heights), extent[dim] // shards_of).reshape((-1,) + (1,) * (len(extent) - dim - 1))

    factor_of = one(*split[0])
    for cut in split[1:]:
        factor_of = factor_of * one(*cut)
    return factor_of


def noise(key, dims, deviation, limit, pieces=(), dtype=jnp.bfloat16):
    loudness = steps_of(key, dims, pieces, -0.22, 0.18) if pieces else 1.0
    result = jax.random.normal(key, dims, jnp.float32) * deviation * loudness
    return jnp.minimum(jnp.maximum(result, -limit), limit).astype(dtype)


def setup_inputs(seed: int = 0) -> dict:
    streams_of = jax.random.split(jax.random.key(seed), 6)
    queries = draw_queries(jax.random.fold_in(streams_of[5], 71), 0)
    image_keys = draw_image_keys(jax.random.fold_in(streams_of[5], 71), 0)
    image_states = noise(streams_of[2], (N_DP, IMG, D), 1.0, 6.0, ((0, 2), (1, 8)))
    value_weight = noise(streams_of[3], (D, KV_HEADS * HD), D ** -0.5, 0.0625, ((0, 8), (1, 2)))
    out_grad = noise(streams_of[4], (N_DP, TEXT, HEADS * HD), 1.0, 6.0, ((0, 2), (1, 8), (2, 2)))
    return dict(queries=queries, image_keys=image_keys, image_states=image_states, value_weight=value_weight, out_grad=out_grad)


def round_low(values):
    return lax.optimization_barrier(values.astype(jnp.bfloat16)).astype(jnp.float32)

def reference(queries, image_keys, image_states, value_weight, out_grad):
    inv_root = 1.0 / math.sqrt(HD)
    kv_columns = KV_HEADS * HD
    text_span = math.gcd(TEXT, 1024)
    hi_prec = lax.Precision.HIGHEST
    query_list = []
    key_list = []
    image_list = []
    weight_acc = jnp.zeros((D, kv_columns), jnp.float32)
    for replica in range(N_DP):
        values = jnp.dot(image_states[replica], value_weight, preferred_element_type=jnp.float32).astype(jnp.bfloat16)
        key_full = image_keys[replica].astype(jnp.float32).reshape(IMG, KV_HEADS, HD)
        value_full = values.astype(jnp.float32).reshape(IMG, KV_HEADS, HD)
        query_blocks = queries[replica].reshape(TEXT // text_span, text_span, KV_HEADS, GROUP, HD)
        grad_blocks = out_grad[replica].reshape(TEXT // text_span, text_span, KV_HEADS, GROUP, HD)

        def text_step(running, blocks):
            key_acc, value_acc = running
            query_f = blocks[0].astype(jnp.float32)
            grad_f = blocks[1].astype(jnp.float32)
            scores = jnp.einsum('tkgd,jkd->tkgj', query_f, key_full, precision=hi_prec) * inv_root
            highest = scores.max(-1, keepdims=True)
            expo = jnp.exp(scores - highest)
            probs = expo / expo.sum(-1, keepdims=True)
            slopes = jnp.einsum('tkgd,jkd->tkgj', grad_f, value_full, precision=hi_prec)
            row_delta = (probs * slopes).sum(-1, keepdims=True)
            dscores = round_low(probs * (slopes - row_delta) * inv_root)
            probs_low = round_low(probs)
            query_part = jnp.einsum('tkgj,jkd->tkgd', dscores, key_full, precision=hi_prec)
            key_acc = key_acc + jnp.einsum('tkgj,tkgd->jkd', dscores, query_f, precision=hi_prec)
            value_acc = value_acc + jnp.einsum('tkgj,tkgd->jkd', probs_low, grad_f, precision=hi_prec)
            return ((key_acc, value_acc), query_part.astype(jnp.bfloat16))
        zero_grad = jnp.zeros((IMG, KV_HEADS, HD), jnp.float32)
        (key_acc, value_acc), query_parts = lax.scan(text_step, (zero_grad, zero_grad), (query_blocks, grad_blocks))
        query_list.append(query_parts.reshape(TEXT, HEADS * HD))
        key_list.append(key_acc.astype(jnp.bfloat16).reshape(IMG, kv_columns))
        value_low = value_acc.astype(jnp.bfloat16).reshape(IMG, kv_columns)
        state_blocks = image_states[replica].reshape(N_SEQ, IMG_DEV, D)
        grad_rows = value_low.reshape(N_SEQ, IMG_DEV, kv_columns)

        def weight_step(total, blocks):
            term = lax.dot_general(blocks[0], blocks[1], (((0,), (0,)), ((), ())), preferred_element_type=jnp.float32)
            return (total + round_low(term), None)
        weight_acc, unused = lax.scan(weight_step, weight_acc, (state_blocks, grad_rows))
        image_acc = jnp.zeros((IMG, D), jnp.float32)
        group_cols = KV_DEV * HD
        for tensor_index in range(N_TENSOR):
            low = tensor_index * group_cols
            term = lax.dot_general(value_low[:, low:low + group_cols], value_weight[:, low:low + group_cols], (((1,), (1,)), ((), ())), preferred_element_type=jnp.float32)
            image_acc = image_acc + round_low(term)
        image_list.append(image_acc.astype(jnp.bfloat16))
    return (jnp.stack(query_list), jnp.stack(key_list), weight_acc.astype(jnp.bfloat16), jnp.stack(image_list))
```

```python
import functools
import math

import jax
import jax.numpy as jnp
from jax import lax
from jax.experimental import pallas as pl
from jax.experimental.pallas import tpu as pltpu
from jax.sharding import PartitionSpec as P

HD = 128
MESH = pl.DeviceIdType.MESH
F32 = jnp.float32
BF16 = jnp.bfloat16


def dot(a, b, a_dim, b_dim):
    return lax.dot_general(a, b, (((a_dim,), (b_dim,)), ((), ())), preferred_element_type=F32)


def kernel(
    n_dp, n_seq, n_t,
    q_ref, k_ref, st_ref, w_ref, og_ref,
    qg_ref, kg_ref, wg_ref, ig_ref,
    keys_all, scol, w_all, probs, vp_acc, vp_send, vp_recv, xp_send, xp_recv,
    vg_all, val_all, kp_acc, kp_send, kp_recv, wg_send, wg_recv, ig_send, ig_recv,
    keys_ss, keys_rs, st_ss, st_rs, w_ss, w_rs, vp_ss, vp_rs, xp_ss, xp_rs,
    vg_ss, vg_rs, val_ss, val_rs, kp_ss, kp_rs, wg_ss, wg_rs, ig_ss, ig_rs,
):
    d, s, t = lax.axis_index("dp"), lax.axis_index("seq"), lax.axis_index("tensor")
    img_dev = k_ref.shape[1]
    image_total = n_seq * img_dev
    text_rows = q_ref.shape[1]
    heads = q_ref.shape[2] // HD
    d_seq = w_ref.shape[0]
    per_t = n_seq // n_t
    inv_root = 1.0 / math.sqrt(HD)

    def plus(a, b, n):
        return lax.rem(a + b, n)

    def minus(a, b, n):
        return lax.rem(a - b + n, n)

    def remote(src, dst, send, recv, device):
        return pltpu.make_async_remote_copy(
            src_ref=src, dst_ref=dst, send_sem=send, recv_sem=recv,
            device_id=device, device_id_type=MESH,
        )

    def over_seq(fn):
        pl.loop(1, n_seq)(fn)

    barrier = pltpu.get_barrier_semaphore()

    @pl.loop(1, n_seq * n_t)
    def _(m):
        pl.semaphore_signal(
            barrier, inc=1,
            device_id={"seq": plus(s, m // n_t, n_seq), "tensor": plus(t, m % n_t, n_t)},
            device_id_type=MESH,
        )

    for kd in range(1, n_dp):
        pl.semaphore_signal(
            barrier, inc=1, device_id={"dp": plus(d, kd, n_dp)}, device_id_type=MESH
        )
    pl.semaphore_wait(barrier, n_seq * n_t - 1 + n_dp - 1)

    def keys_copy(k):
        return remote(k_ref.at[0], keys_all.at[s], keys_ss.at[k], keys_rs.at[k],
                      {"seq": plus(s, k, n_seq)})

    @over_seq
    def _(k):
        keys_copy(k).start()

    def st_copy(k):
        to = plus(s, k, n_seq)
        cols = pl.ds(pl.multiple_of(to * d_seq, d_seq), d_seq)
        return remote(st_ref.at[0, :, cols], scol.at[s], st_ss.at[k], st_rs.at[k], {"seq": to})

    @over_seq
    def _(k):
        st_copy(k).start()

    def w_copy(k):
        return remote(w_ref, w_all.at[t], w_ss.at[k], w_rs.at[k], {"tensor": plus(t, k, n_t)})

    for k in range(1, n_t):
        w_copy(k).start()

    keys_all[s] = k_ref[0]
    scol[s] = st_ref[0, :, pl.ds(pl.multiple_of(s * d_seq, d_seq), d_seq)]
    w_all[t] = w_ref[...]

    def landed(buffer, send, recv, k):
        source = buffer.at[minus(s, k, n_seq)]
        return remote(source, source, send.at[k], recv.at[k], {"seq": plus(s, k, n_seq)})

    @over_seq
    def _(k):
        landed(keys_all, keys_ss, keys_rs, k).wait_recv()

    vp_acc[...] = jnp.zeros_like(vp_acc)

    @pl.loop(0, heads)
    def _(h):
        cols = pl.ds(pl.multiple_of(h * HD, HD), HD)
        keys = keys_all[...].reshape(image_total, HD)
        raw = dot(keys, q_ref[0, :, cols], 1, 1) * inv_root
        expo = jnp.exp(raw - raw.max(0, keepdims=True))
        p = expo * (1.0 / expo.sum(0, keepdims=True))
        probs[h] = p
        vp_acc[...] += dot(p.astype(BF16), og_ref[0, :, cols], 1, 0)

    vp_send[...] = vp_acc[...].astype(BF16).reshape(n_seq, img_dev, HD)

    def scatter_copy(src, dst, send, recv, k):
        to = plus(s, k, n_seq)
        return remote(src.at[to], dst.at[s], send.at[k], recv.at[k], {"seq": to})

    @over_seq
    def _(k):
        scatter_copy(vp_send, vp_recv, vp_ss, vp_rs, k).start()

    vp_recv[s] = vp_send[s]

    @over_seq
    def _(k):
        landed(vp_recv, vp_ss, vp_rs, k).wait_recv()

    vg_all[t, s] = vp_recv[...].astype(F32).sum(0).astype(BF16)

    def vg_copy(m):
        return remote(
            vg_all.at[t, s], vg_all.at[t, s], vg_ss.at[m], vg_rs.at[m],
            {"seq": plus(s, m // n_t, n_seq), "tensor": plus(t, m % n_t, n_t)},
        )

    @pl.loop(1, n_seq * n_t)
    def _(m):
        vg_copy(m).start()

    @over_seq
    def _(k):
        landed(scol, st_ss, st_rs, k).wait_recv()

    states = scol[...].reshape(image_total, d_seq)
    xp_send[...] = dot(states, w_ref[...], 1, 0).reshape(n_seq, img_dev, HD)

    @over_seq
    def _(k):
        scatter_copy(xp_send, xp_recv, xp_ss, xp_rs, k).start()

    xp_recv[s] = xp_send[s]

    @pl.loop(1, n_seq * n_t)
    def _(m):
        source = vg_all.at[minus(t, m % n_t, n_t), minus(s, m // n_t, n_seq)]
        remote(source, source, vg_ss.at[m], vg_rs.at[m],
               {"seq": plus(s, m // n_t, n_seq), "tensor": plus(t, m % n_t, n_t)}).wait_recv()

    vg_own = vg_all[t].reshape(image_total, HD)
    wg_send[...] = dot(scol[...].reshape(image_total, d_seq), vg_own, 0, 0).astype(BF16)

    def wg_copy(k):
        return remote(wg_send, wg_recv.at[d], wg_ss.at[k], wg_rs.at[k], {"dp": plus(d, k, n_dp)})

    for k in range(1, n_dp):
        wg_copy(k).start()

    for k in range(1, n_t):
        source = w_all.at[minus(t, k, n_t)]
        remote(source, source, w_ss.at[k], w_rs.at[k], {"tensor": plus(t, k, n_t)}).wait_recv()

    def image_term(c):
        rows = jnp.concatenate([vg_all[c, j * n_t + t] for j in range(per_t)], axis=0)
        return dot(rows, w_all[c], 1, 1).astype(BF16).astype(F32)

    total = image_term(0)
    for c in range(1, n_t):
        total = total + image_term(c)
    ig_send[...] = total.astype(BF16).reshape(per_t, img_dev, d_seq)

    to_t = s // per_t
    slot = pl.ds(pl.multiple_of(lax.rem(s, per_t) * d_seq, d_seq), d_seq)

    def ig_copy(j):
        return remote(ig_send.at[j], ig_recv.at[:, slot], ig_ss.at[j], ig_rs.at[lax.rem(s, per_t)],
                      {"seq": j * n_t + t, "tensor": to_t})

    def ig_stays(j):
        return jnp.logical_and(j * n_t + t == s, to_t == t)

    for j in range(per_t):
        @pl.when(jnp.logical_not(ig_stays(j)))
        def _():
            ig_copy(j).start()

        @pl.when(ig_stays(j))
        def _():
            ig_recv[:, slot] = ig_send[j]

    @over_seq
    def _(k):
        landed(xp_recv, xp_ss, xp_rs, k).wait_recv()

    val_all[s] = xp_recv[...].sum(0).astype(BF16)

    def val_copy(k):
        return remote(val_all.at[s], val_all.at[s], val_ss.at[k], val_rs.at[k],
                      {"seq": plus(s, k, n_seq)})

    @over_seq
    def _(k):
        val_copy(k).start()

    @over_seq
    def _(k):
        landed(val_all, val_ss, val_rs, k).wait_recv()

    kp_acc[...] = jnp.zeros_like(kp_acc)

    @pl.loop(0, heads)
    def _(h):
        cols = pl.ds(pl.multiple_of(h * HD, HD), HD)
        slopes = dot(val_all[...].reshape(image_total, HD), og_ref[0, :, cols], 1, 1)
        p = probs[h]
        delta = (p * slopes).sum(0, keepdims=True)
        ds = (p * (slopes - delta) * inv_root).astype(BF16)
        kp_acc[...] += dot(ds, q_ref[0, :, cols], 1, 0)
        keys = keys_all[...].reshape(image_total, HD)
        qg_ref[0, :, cols] = dot(ds, keys, 0, 0).astype(BF16)

    kp_send[...] = kp_acc[...].astype(BF16).reshape(n_seq, img_dev, HD)

    @over_seq
    def _(k):
        scatter_copy(kp_send, kp_recv, kp_ss, kp_rs, k).start()

    kp_recv[s] = kp_send[s]

    wg_total = wg_send[...].astype(F32)
    for k in range(1, n_dp):
        source = wg_recv.at[minus(d, k, n_dp)]
        remote(source, source, wg_ss.at[k], wg_rs.at[k], {"dp": plus(d, k, n_dp)}).wait_recv()
        wg_total = wg_total + wg_recv[minus(d, k, n_dp)].astype(F32)
    wg_ref[...] = wg_total.astype(BF16)

    for j in range(per_t):
        from_s = t * per_t + j
        from_t = lax.rem(s, n_t)

        @pl.when(jnp.logical_not(jnp.logical_and(from_s == s, from_t == t)))
        def _():
            place = ig_recv.at[:, pl.ds(j * d_seq, d_seq)]
            remote(ig_send.at[0], place, ig_ss.at[j], ig_rs.at[j],
                   {"seq": from_s, "tensor": from_t}).wait_recv()

    ig_ref[0] = ig_recv[...]

    @over_seq
    def _(k):
        landed(kp_recv, kp_ss, kp_rs, k).wait_recv()

    kg_ref[0] = kp_recv[...].astype(F32).sum(0).astype(BF16)

    @over_seq
    def _(k):
        keys_copy(k).wait_send()
        st_copy(k).wait_send()
        scatter_copy(vp_send, vp_recv, vp_ss, vp_rs, k).wait_send()
        scatter_copy(xp_send, xp_recv, xp_ss, xp_rs, k).wait_send()
        val_copy(k).wait_send()
        scatter_copy(kp_send, kp_recv, kp_ss, kp_rs, k).wait_send()

    @pl.loop(1, n_seq * n_t)
    def _(m):
        vg_copy(m).wait_send()

    for k in range(1, n_t):
        w_copy(k).wait_send()
    for k in range(1, n_dp):
        wg_copy(k).wait_send()
    for j in range(per_t):
        @pl.when(jnp.logical_not(ig_stays(j)))
        def _():
            ig_copy(j).wait_send()


def on_device(n_dp, n_seq, n_t, queries, image_keys, image_states, value_weight, out_grad):
    img_dev = image_keys.shape[1]
    image_total = n_seq * img_dev
    text_rows = queries.shape[1]
    heads = queries.shape[2] // HD
    d_model = image_states.shape[2]
    d_seq = value_weight.shape[0]
    d_t = d_model // n_t
    per_t = n_seq // n_t
    vmem = pltpu.VMEM
    rows = (n_seq, img_dev, HD)
    scratch = [
        vmem(rows, BF16),
        vmem((n_seq, img_dev, d_seq), BF16),
        vmem((n_t, d_seq, HD), BF16),
        vmem((heads, image_total, text_rows), F32),
        vmem((image_total, HD), F32),
        vmem(rows, BF16),
        vmem(rows, BF16),
        vmem(rows, F32),
        vmem(rows, F32),
        vmem((n_t,) + rows, BF16),
        vmem(rows, BF16),
        vmem((image_total, HD), F32),
        vmem(rows, BF16),
        vmem(rows, BF16),
        vmem((d_seq, HD), BF16),
        vmem((n_dp, d_seq, HD), BF16),
        vmem((per_t, img_dev, d_seq), BF16),
        vmem((img_dev, d_t), BF16),
    ]
    counts = [n_seq, n_seq, n_t, n_seq, n_seq, n_seq * n_t, n_seq, n_seq, n_dp, per_t]
    sems = [pltpu.SemaphoreType.DMA((c,)) for c in counts for _ in range(2)]
    spec = pl.BlockSpec(memory_space=pltpu.VMEM)
    return pl.pallas_call(
        functools.partial(kernel, n_dp, n_seq, n_t),
        out_shape=(
            jax.ShapeDtypeStruct(queries.shape, BF16),
            jax.ShapeDtypeStruct(image_keys.shape, BF16),
            jax.ShapeDtypeStruct(value_weight.shape, BF16),
            jax.ShapeDtypeStruct((1, img_dev, d_t), BF16),
        ),
        in_specs=[spec] * 5,
        out_specs=(spec,) * 4,
        scratch_shapes=scratch + sems,
        compiler_params=pltpu.CompilerParams(
            collective_id=0, has_side_effects=True, vmem_limit_bytes=48 * 1024 * 1024
        ),
    )(queries, image_keys, image_states, value_weight, out_grad)


def solution(mesh):
    in_specs = (
        P("dp", "seq", "tensor"),
        P("dp", "seq", "tensor"),
        P("dp", "seq", None),
        P("seq", "tensor"),
        P("dp", "seq", "tensor"),
    )
    out_specs = (
        P("dp", "seq", "tensor"),
        P("dp", "seq", "tensor"),
        P("seq", "tensor"),
        P("dp", "seq", "tensor"),
    )
    sizes = (mesh.shape["dp"], mesh.shape["seq"], mesh.shape["tensor"])
    return jax.shard_map(
        functools.partial(on_device, *sizes),
        mesh=mesh, in_specs=in_specs, out_specs=out_specs, check_vma=False,
    )
```

```python
import functools
import math

import jax
import jax.numpy as jnp
from jax import lax
from jax.experimental import pallas as pl
from jax.experimental.pallas import tpu as pltpu
from jax.sharding import PartitionSpec as P

HD = 128
MESH = pl.DeviceIdType.MESH
F32 = jnp.float32
BF16 = jnp.bfloat16
XP = jnp.bfloat16


def dot(a, b, a_dim, b_dim):
    return lax.dot_general(a, b, (((a_dim,), (b_dim,)), ((), ())), preferred_element_type=F32)


def kernel(
    n_dp, n_seq, n_t,
    q_hbm, k_hbm, st_hbm, w_hbm, og_hbm,
    qg_hbm, kg_hbm, wg_hbm, ig_hbm,
    qg_ref, kg_ref, wg_ref, ig_ref, q_ref, og_ref, keys_all, scol, w_all, probs, vp_acc, vp_send, vp_recv, xp_send, xp_recv,
    vg_all, val_all, kp_acc, kp_send, kp_recv, wg_send, wg_recv, ig_send, ig_recv,
    out_sem, in_sem, keys_ss, keys_rs, st_ss, st_rs, w_ss, w_rs, vp_ss, vp_rs, xp_ss, xp_rs,
    vg_ss, vg_rs, val_ss, val_rs, kp_ss, kp_rs, wg_ss, wg_rs, ig_ss, ig_rs,
):
    d, s, t = lax.axis_index("dp"), lax.axis_index("seq"), lax.axis_index("tensor")
    img_dev = k_hbm.shape[1]
    image_total = n_seq * img_dev
    text_rows = q_hbm.shape[1]
    heads = q_hbm.shape[2] // HD
    d_seq = w_hbm.shape[0]
    per_t = n_seq // n_t
    inv_root = 1.0 / math.sqrt(HD)

    def plus(a, b, n):
        return lax.rem(a + b, n)

    def minus(a, b, n):
        return lax.rem(a - b + n, n)

    def remote(src, dst, send, recv, device):
        return pltpu.make_async_remote_copy(
            src_ref=src, dst_ref=dst, send_sem=send, recv_sem=recv,
            device_id=device, device_id_type=MESH,
        )

    def over_seq(fn):
        pl.loop(1, n_seq)(fn)

    parts = n_t if d_seq % (n_t * 128) == 0 else 1
    width = d_seq // parts
    part = t % parts

    def cols_of(seq_index):
        return pl.ds(pl.multiple_of(seq_index * d_seq + part * width, width), width)

    def rows_of(c):
        return pl.ds(pl.multiple_of((c % parts) * width, width), width)

    locals_in = [
        pltpu.make_async_copy(k_hbm.at[0], keys_all.at[s], in_sem.at[0]),
        pltpu.make_async_copy(q_hbm, q_ref, in_sem.at[1]),
        pltpu.make_async_copy(og_hbm, og_ref, in_sem.at[2]),
        pltpu.make_async_copy(w_hbm, w_all.at[t], in_sem.at[3]),
        pltpu.make_async_copy(st_hbm.at[0, :, cols_of(s)], scol.at[s], in_sem.at[4]),
    ]

    barrier = pltpu.get_barrier_semaphore()

    @pl.loop(1, n_seq * n_t)
    def _(m):
        pl.semaphore_signal(
            barrier, inc=1,
            device_id={"seq": plus(s, m // n_t, n_seq), "tensor": plus(t, m % n_t, n_t)},
            device_id_type=MESH,
        )

    for kd in range(1, n_dp):
        for kt in range(parts):
            pl.semaphore_signal(
                barrier, inc=1,
                device_id={"dp": plus(d, kd, n_dp), "tensor": plus(t, kt, n_t)},
                device_id_type=MESH,
            )
    for copy in locals_in:
        copy.start()
    pl.semaphore_wait(barrier, n_seq * n_t - 1 + (n_dp - 1) * parts)

    def keys_copy(k):
        return remote(k_hbm.at[0], keys_all.at[s], keys_ss.at[k], keys_rs.at[k],
                      {"seq": plus(s, k, n_seq)})

    @over_seq
    def _(k):
        keys_copy(k).start()

    def st_copy(k):
        to = plus(s, k, n_seq)
        return remote(st_hbm.at[0, :, cols_of(to)], scol.at[s], st_ss.at[k], st_rs.at[k], {"seq": to})

    @over_seq
    def _(k):
        st_copy(k).start()

    def w_copy(k):
        to = plus(t, k, n_t)
        return remote(w_hbm.at[rows_of(to)], w_all.at[t, rows_of(to)], w_ss.at[k], w_rs.at[k],
                      {"tensor": to})

    def w_arrived():
        for k in range(1, n_t):
            place = w_all.at[minus(t, k, n_t), rows_of(t)]
            remote(place, place, w_ss.at[k], w_rs.at[k], {"tensor": plus(t, k, n_t)}).wait_recv()

    for k in range(1, n_t):
        w_copy(k).start()

    for copy in locals_in:
        copy.wait()

    def landed(buffer, send, recv, k):
        source = buffer.at[minus(s, k, n_seq)]
        return remote(source, source, send.at[k], recv.at[k], {"seq": plus(s, k, n_seq)})

    @over_seq
    def _(k):
        landed(keys_all, keys_ss, keys_rs, k).wait_recv()

    vp_acc[...] = jnp.zeros_like(vp_acc)

    @pl.loop(0, heads, unroll=heads)
    def _(h):
        cols = pl.ds(pl.multiple_of(h * HD, HD), HD)
        keys = keys_all[...].reshape(image_total, HD)
        raw = dot(keys, q_ref[0, :, cols], 1, 1) * inv_root
        expo = jnp.exp(raw - raw.max(0, keepdims=True))
        p = expo * (1.0 / expo.sum(0, keepdims=True))
        probs[h] = p
        vp_acc[...] += dot(p.astype(BF16), og_ref[0, :, cols], 1, 0)

    vp_send[...] = vp_acc[...].astype(BF16).reshape(n_seq, img_dev, HD)

    def scatter_copy(src, dst, send, recv, k):
        to = plus(s, k, n_seq)
        return remote(src.at[to], dst.at[s], send.at[k], recv.at[k], {"seq": to})

    @over_seq
    def _(k):
        scatter_copy(vp_send, vp_recv, vp_ss, vp_rs, k).start()

    vp_recv[s] = vp_send[s]

    @over_seq
    def _(k):
        landed(scol, st_ss, st_rs, k).wait_recv()

    if parts > 1:
        w_arrived()

    def weight_part(n):
        return jnp.concatenate([w_all[plus(t, kt, n_t), rows_of(t)] for kt in range(n)], axis=1)

    states = scol[...].reshape(image_total, width)
    sums = dot(states, weight_part(parts), 1, 0)
    for kt in range(parts):
        xp_send[kt] = (
            sums[:, kt * HD : (kt + 1) * HD].reshape(n_seq, img_dev, HD).astype(xp_send.dtype)
        )

    def xp_copy(kt, k):
        to = plus(s, k, n_seq)
        return remote(xp_send.at[kt, to], xp_recv.at[part, s], xp_ss.at[kt, k], xp_rs.at[kt, k],
                      {"seq": to, "tensor": plus(t, kt, n_t)})

    def xp_arrived(kt, k):
        place = xp_recv.at[minus(t, kt, n_t) % parts, minus(s, k, n_seq)]
        return remote(place, place, xp_ss.at[kt, k], xp_rs.at[kt, k],
                      {"seq": plus(s, k, n_seq), "tensor": plus(t, kt, n_t)})

    for kt in range(parts):
        @pl.loop(0 if kt else 1, n_seq)
        def _(k):
            xp_copy(kt, k).start()

    xp_recv[part, s] = xp_send[0, s]

    @over_seq
    def _(k):
        landed(vp_recv, vp_ss, vp_rs, k).wait_recv()

    vg_all[t, s] = vp_recv[...].astype(F32).sum(0).astype(BF16)

    def vg_copy(m):
        return remote(
            vg_all.at[t, s], vg_all.at[t, s], vg_ss.at[m], vg_rs.at[m],
            {"seq": plus(s, m // n_t, n_seq), "tensor": plus(t, m % n_t, n_t)},
        )

    def vg_goes(m):
        if parts > 1:
            return m > 0
        return jnp.logical_or(m % n_t == 0, lax.rem(s, n_t) == plus(t, m % n_t, n_t))

    @pl.loop(1, n_seq * n_t)
    def _(m):
        @pl.when(vg_goes(m))
        def _():
            vg_copy(m).start()

    for kt in range(parts):
        @pl.loop(0 if kt else 1, n_seq)
        def _(k):
            xp_arrived(kt, k).wait_recv()

    val_all[s] = xp_recv[...].astype(F32).sum((0, 1)).astype(BF16)

    def val_copy(k):
        return remote(val_all.at[s], val_all.at[s], val_ss.at[k], val_rs.at[k],
                      {"seq": plus(s, k, n_seq)})

    @over_seq
    def _(k):
        val_copy(k).start()

    @pl.loop(1, n_seq * n_t)
    def _(m):
        from_s = minus(s, m // n_t, n_seq)

        @pl.when(m > 0 if parts > 1 else jnp.logical_or(m % n_t == 0, lax.rem(from_s, n_t) == t))
        def _():
            source = vg_all.at[minus(t, m % n_t, n_t), from_s]
            remote(source, source, vg_ss.at[m], vg_rs.at[m],
                   {"seq": plus(s, m // n_t, n_seq), "tensor": plus(t, m % n_t, n_t)}).wait_recv()

    def grads_of(n):
        return jnp.concatenate(
            [vg_all[plus(t, kt, n_t)].reshape(image_total, HD) for kt in range(n)], axis=1
        )

    terms = dot(scol[...].reshape(image_total, width), grads_of(parts), 0, 0)
    for kt in range(parts):
        wg_send[kt] = terms[:, kt * HD : (kt + 1) * HD].astype(BF16)

    def wg_copy(kd, kt):
        return remote(wg_send.at[kt], wg_recv.at[d, rows_of(t)], wg_ss.at[kd, kt],
                      wg_rs.at[kd, kt],
                      {"dp": plus(d, kd, n_dp), "tensor": plus(t, kt, n_t)})

    wg_moves = [(kd, kt) for kd in range(n_dp) for kt in range(parts) if kd + kt > 0]
    for kd, kt in wg_moves:
        wg_copy(kd, kt).start()
    wg_recv[d, rows_of(t)] = wg_send[0]

    if parts == 1:
        w_arrived()

    def image_term(c):
        rows = jnp.concatenate([vg_all[c, j * n_t + t] for j in range(per_t)], axis=0)
        return dot(rows, w_all[c], 1, 1).astype(BF16).astype(F32)

    if parts > 1:
        total = dot(grads_of(n_t), weight_part(n_t), 1, 1)
    else:
        total = image_term(0)
        for c in range(1, n_t):
            total = total + image_term(c)
    blocks = ig_send.shape[0]
    ig_send[...] = total.astype(BF16).reshape(blocks, img_dev, width)

    to_t = s // per_t
    slot = cols_of(lax.rem(s, per_t))
    place_in = lax.rem(s, per_t) * parts + part

    def row_block(j):
        return j if parts > 1 else j * n_t + t

    def ig_copy(j):
        return remote(ig_send.at[j], ig_recv.at[:, slot], ig_ss.at[j], ig_rs.at[place_in],
                      {"seq": row_block(j), "tensor": to_t})

    def ig_stays(j):
        return jnp.logical_and(row_block(j) == s, to_t == t)

    for j in range(blocks):
        @pl.when(jnp.logical_not(ig_stays(j)))
        def _():
            ig_copy(j).start()

        @pl.when(ig_stays(j))
        def _():
            ig_recv[:, slot] = ig_send[j]

    @over_seq
    def _(k):
        landed(val_all, val_ss, val_rs, k).wait_recv()

    kp_acc[...] = jnp.zeros_like(kp_acc)

    @pl.loop(0, heads, unroll=heads)
    def _(h):
        cols = pl.ds(pl.multiple_of(h * HD, HD), HD)
        slopes = dot(val_all[...].reshape(image_total, HD), og_ref[0, :, cols], 1, 1)
        p = probs[h]
        delta = (p * slopes).sum(0, keepdims=True)
        ds = (p * (slopes - delta) * inv_root).astype(BF16)
        kp_acc[...] += dot(ds, q_ref[0, :, cols], 1, 0)
        keys = keys_all[...].reshape(image_total, HD)
        qg_ref[0, :, cols] = dot(ds, keys, 0, 0).astype(BF16)

    qg_out = pltpu.make_async_copy(qg_ref, qg_hbm, out_sem.at[0])
    qg_out.start()
    kp_send[...] = kp_acc[...].astype(BF16).reshape(n_seq, img_dev, HD)

    @over_seq
    def _(k):
        scatter_copy(kp_send, kp_recv, kp_ss, kp_rs, k).start()

    kp_recv[s] = kp_send[s]

    for kd, kt in wg_moves:
        place = wg_recv.at[minus(d, kd, n_dp), rows_of(minus(t, kt, n_t))]
        remote(place, place, wg_ss.at[kd, kt], wg_rs.at[kd, kt],
               {"dp": plus(d, kd, n_dp), "tensor": plus(t, kt, n_t)}).wait_recv()
    wg_ref[...] = wg_recv[...].astype(F32).sum(0).astype(BF16)
    wg_out = pltpu.make_async_copy(wg_ref, wg_hbm, out_sem.at[1])
    wg_out.start()

    for j in range(per_t * parts):
        from_s = t * per_t + j // parts
        from_t = j % parts if parts > 1 else lax.rem(s, n_t)

        @pl.when(jnp.logical_not(jnp.logical_and(from_s == s, from_t == t)))
        def _():
            place = ig_recv.at[:, pl.ds(j * width, width)]
            remote(ig_send.at[0], place, ig_ss.at[j], ig_rs.at[j],
                   {"seq": from_s, "tensor": from_t}).wait_recv()

    ig_out = pltpu.make_async_copy(ig_recv, ig_hbm.at[0], out_sem.at[2])
    ig_out.start()

    @over_seq
    def _(k):
        landed(kp_recv, kp_ss, kp_rs, k).wait_recv()

    kg_ref[0] = kp_recv[...].astype(F32).sum(0).astype(BF16)

    kg_out = pltpu.make_async_copy(kg_ref, kg_hbm, out_sem.at[3])
    kg_out.start()

    for kt in range(parts):
        @pl.loop(0 if kt else 1, n_seq)
        def _(k):
            xp_copy(kt, k).wait_send()

    @over_seq
    def _(k):
        keys_copy(k).wait_send()
        st_copy(k).wait_send()
        scatter_copy(vp_send, vp_recv, vp_ss, vp_rs, k).wait_send()
        val_copy(k).wait_send()
        scatter_copy(kp_send, kp_recv, kp_ss, kp_rs, k).wait_send()

    @pl.loop(1, n_seq * n_t)
    def _(m):
        @pl.when(vg_goes(m))
        def _():
            vg_copy(m).wait_send()

    for k in range(1, n_t):
        w_copy(k).wait_send()
    for kd, kt in wg_moves:
        wg_copy(kd, kt).wait_send()
    for j in range(blocks):
        @pl.when(jnp.logical_not(ig_stays(j)))
        def _():
            ig_copy(j).wait_send()
    for copy in (qg_out, wg_out, ig_out, kg_out):
        copy.wait()


def write_out(*refs):
    copies = [pltpu.make_async_copy(refs[i], refs[4 + i], refs[8].at[i]) for i in range(4)]
    for copy in copies:
        copy.start()
    for copy in copies:
        copy.wait()


def on_device(n_dp, n_seq, n_t, queries, image_keys, image_states, value_weight, out_grad):
    img_dev = image_keys.shape[1]
    image_total = n_seq * img_dev
    text_rows = queries.shape[1]
    heads = queries.shape[2] // HD
    d_model = image_states.shape[2]
    d_seq = value_weight.shape[0]
    d_t = d_model // n_t
    per_t = n_seq // n_t
    parts = n_t if d_seq % (n_t * 128) == 0 else 1
    width = d_seq // parts
    vmem = pltpu.VMEM
    rows = (n_seq, img_dev, HD)
    scratch = [
        vmem(queries.shape, BF16),
        vmem(image_keys.shape, BF16),
        vmem(value_weight.shape, BF16),
        vmem((1, img_dev, d_t), BF16),
        vmem(queries.shape, BF16),
        vmem(out_grad.shape, BF16),
        vmem(rows, BF16),
        vmem((n_seq, img_dev, width), BF16),
        vmem((n_t, d_seq, HD), BF16),
        vmem((heads, image_total, text_rows), F32),
        vmem((image_total, HD), F32),
        vmem(rows, BF16),
        vmem(rows, BF16),
        vmem((parts,) + rows, XP),
        vmem((parts,) + rows, XP),
        vmem((n_t,) + rows, BF16),
        vmem(rows, BF16),
        vmem((image_total, HD), F32),
        vmem(rows, BF16),
        vmem(rows, BF16),
        vmem((parts, width, HD), BF16),
        vmem((n_dp, d_seq, HD), BF16),
        vmem((per_t * parts, img_dev, width), BF16),
        vmem((img_dev, d_t), BF16),
    ]
    counts = [
        (n_seq,), (n_seq,), (n_t,), (n_seq,), (parts, n_seq), (n_seq * n_t,), (n_seq,), (n_seq,),
        (n_dp, parts), (per_t * parts,),
    ]
    sems = [pltpu.SemaphoreType.DMA((4,))] + [pltpu.SemaphoreType.DMA((5,))] + [pltpu.SemaphoreType.DMA(c) for c in counts for _ in range(2)]
    spec = pl.BlockSpec(memory_space=pltpu.VMEM)
    grads = pl.pallas_call(
        functools.partial(kernel, n_dp, n_seq, n_t),
        out_shape=(
            jax.ShapeDtypeStruct(queries.shape, BF16),
            jax.ShapeDtypeStruct(image_keys.shape, BF16),
            jax.ShapeDtypeStruct(value_weight.shape, BF16),
            jax.ShapeDtypeStruct((1, img_dev, d_t), BF16),
        ),
        in_specs=[pl.BlockSpec(memory_space=pltpu.HBM)] * 5,
        out_specs=(pl.BlockSpec(memory_space=pltpu.HBM),) * 4,
        scratch_shapes=scratch + sems,
        compiler_params=pltpu.CompilerParams(
            collective_id=0, has_side_effects=True, vmem_limit_bytes=63 * 1024 * 1024
        ),
    )(queries, image_keys, image_states, value_weight, out_grad)
    return pl.pallas_call(
        write_out,
        out_shape=tuple(jax.ShapeDtypeStruct(g.shape, g.dtype) for g in grads),
        in_specs=[spec] * 4,
        out_specs=(pl.BlockSpec(memory_space=pltpu.HBM),) * 4,
        scratch_shapes=[pltpu.SemaphoreType.DMA((4,))],
    )(*grads)


def solution(mesh):
    in_specs = (
        P("dp", "seq", "tensor"),
        P("dp", "seq", "tensor"),
        P("dp", "seq", None),
        P("seq", "tensor"),
        P("dp", "seq", "tensor"),
    )
    out_specs = (
        P("dp", "seq", "tensor"),
        P("dp", "seq", "tensor"),
        P("seq", "tensor"),
        P("dp", "seq", "tensor"),
    )
    sizes = (mesh.shape["dp"], mesh.shape["seq"], mesh.shape["tensor"])
    return jax.shard_map(
        functools.partial(on_device, *sizes),
        mesh=mesh, in_specs=in_specs, out_specs=out_specs, check_vma=False,
    )
```

```python
import functools
import math

import jax
import jax.numpy as jnp
from jax import lax
from jax.experimental import pallas as pl
from jax.experimental.pallas import tpu as pltpu
from jax.sharding import PartitionSpec as P

HD = 128
MESH = pl.DeviceIdType.MESH
F32 = jnp.float32
BF16 = jnp.bfloat16
XP = jnp.bfloat16


def dot(a, b, a_dim, b_dim):
    return lax.dot_general(a, b, (((a_dim,), (b_dim,)), ((), ())), preferred_element_type=F32)


def kernel(
    n_dp, n_seq, n_t,
    q_hbm, k_hbm, st_hbm, w_hbm, og_hbm,
    qg_hbm, kg_hbm, wg_hbm, ig_hbm,
    qg_ref, kg_ref, wg_ref, ig_ref, q_ref, og_ref, keys_all, scol, turned, w_all, probs, vp_acc, vp_send, vp_recv, xp_send, xp_recv,
    vg_all, val_all, kp_acc, kp_send, kp_recv, wg_send, wg_recv, ig_send, ig_recv,
    out_sem, in_sem, keys_ss, keys_rs, st_ss, st_rs, w_ss, w_rs, vp_ss, vp_rs, xp_ss, xp_rs,
    vg_ss, vg_rs, val_ss, val_rs, kp_ss, kp_rs, wg_ss, wg_rs, ig_ss, ig_rs,
):
    d, s, t = lax.axis_index("dp"), lax.axis_index("seq"), lax.axis_index("tensor")
    img_dev = k_hbm.shape[1]
    image_total = n_seq * img_dev
    text_rows = q_hbm.shape[1]
    heads = q_hbm.shape[2] // HD
    d_seq = w_hbm.shape[0]
    per_t = n_seq // n_t
    inv_root = 1.0 / math.sqrt(HD)

    def plus(a, b, n):
        return lax.rem(a + b, n)

    def minus(a, b, n):
        return lax.rem(a - b + n, n)

    def remote(src, dst, send, recv, device):
        return pltpu.make_async_remote_copy(
            src_ref=src, dst_ref=dst, send_sem=send, recv_sem=recv,
            device_id=device, device_id_type=MESH,
        )

    def over_seq(fn):
        pl.loop(1, n_seq)(fn)

    parts = n_t if d_seq % (n_t * 128) == 0 else 1
    width = d_seq // parts
    part = t % parts

    def cols_of(seq_index):
        return pl.ds(pl.multiple_of(seq_index * d_seq + part * width, width), width)

    def rows_of(c):
        return pl.ds(pl.multiple_of((c % parts) * width, width), width)

    locals_in = [
        pltpu.make_async_copy(k_hbm.at[0], keys_all.at[s], in_sem.at[0]),
        pltpu.make_async_copy(q_hbm, q_ref, in_sem.at[1]),
        pltpu.make_async_copy(og_hbm, og_ref, in_sem.at[2]),
        pltpu.make_async_copy(w_hbm, w_all.at[t], in_sem.at[3]),
        pltpu.make_async_copy(st_hbm.at[0, :, cols_of(s)], scol.at[s], in_sem.at[4]),
    ]

    barrier = pltpu.get_barrier_semaphore()

    @pl.loop(1, n_seq * n_t)
    def _(m):
        pl.semaphore_signal(
            barrier, inc=1,
            device_id={"seq": plus(s, m // n_t, n_seq), "tensor": plus(t, m % n_t, n_t)},
            device_id_type=MESH,
        )

    for kd in range(1, n_dp):
        for kt in range(parts):
            pl.semaphore_signal(
                barrier, inc=1,
                device_id={"dp": plus(d, kd, n_dp), "tensor": plus(t, kt, n_t)},
                device_id_type=MESH,
            )
    for copy in locals_in:
        copy.start()
    pl.semaphore_wait(barrier, n_seq * n_t - 1 + (n_dp - 1) * parts)

    def keys_copy(k):
        return remote(k_hbm.at[0], keys_all.at[s], keys_ss.at[k], keys_rs.at[k],
                      {"seq": plus(s, k, n_seq)})

    @over_seq
    def _(k):
        keys_copy(k).start()

    def st_copy(k):
        to = plus(s, k, n_seq)
        return remote(st_hbm.at[0, :, cols_of(to)], scol.at[s], st_ss.at[k], st_rs.at[k], {"seq": to})

    @over_seq
    def _(k):
        st_copy(k).start()

    def w_copy(k):
        to = plus(t, k, n_t)
        return remote(w_hbm.at[rows_of(to)], w_all.at[t, rows_of(to)], w_ss.at[k], w_rs.at[k],
                      {"tensor": to})

    def w_arrived():
        for k in range(1, n_t):
            place = w_all.at[minus(t, k, n_t), rows_of(t)]
            remote(place, place, w_ss.at[k], w_rs.at[k], {"tensor": plus(t, k, n_t)}).wait_recv()

    for k in range(1, n_t):
        w_copy(k).start()

    for copy in locals_in:
        copy.wait()

    def landed(buffer, send, recv, k):
        source = buffer.at[minus(s, k, n_seq)]
        return remote(source, source, send.at[k], recv.at[k], {"seq": plus(s, k, n_seq)})

    @over_seq
    def _(k):
        landed(keys_all, keys_ss, keys_rs, k).wait_recv()

    vp_acc[...] = jnp.zeros_like(vp_acc)

    @pl.loop(0, heads, unroll=heads)
    def _(h):
        cols = pl.ds(pl.multiple_of(h * HD, HD), HD)
        keys = keys_all[...].reshape(image_total, HD)
        raw = dot(keys, q_ref[0, :, cols], 1, 1) * inv_root
        expo = jnp.exp(raw - raw.max(0, keepdims=True))
        p = expo * (1.0 / expo.sum(0, keepdims=True))
        probs[h] = p
        vp_acc[...] += dot(p.astype(BF16), og_ref[0, :, cols], 1, 0)

    vp_send[...] = vp_acc[...].astype(BF16).reshape(n_seq, img_dev, HD)

    def scatter_copy(src, dst, send, recv, k):
        to = plus(s, k, n_seq)
        return remote(src.at[to], dst.at[s], send.at[k], recv.at[k], {"seq": to})

    @over_seq
    def _(k):
        scatter_copy(vp_send, vp_recv, vp_ss, vp_rs, k).start()

    vp_recv[s] = vp_send[s]

    @over_seq
    def _(k):
        landed(scol, st_ss, st_rs, k).wait_recv()

    if parts > 1:
        w_arrived()

    def weight_part(n):
        return jnp.concatenate([w_all[plus(t, kt, n_t), rows_of(t)] for kt in range(n)], axis=1)

    states = scol[...].reshape(image_total, width)
    sums = dot(states, weight_part(parts), 1, 0)
    for kt in range(parts):
        xp_send[kt] = (
            sums[:, kt * HD : (kt + 1) * HD].reshape(n_seq, img_dev, HD).astype(xp_send.dtype)
        )

    def xp_copy(kt, k):
        to = plus(s, k, n_seq)
        return remote(xp_send.at[kt, to], xp_recv.at[part, s], xp_ss.at[kt, k], xp_rs.at[kt, k],
                      {"seq": to, "tensor": plus(t, kt, n_t)})

    def xp_arrived(kt, k):
        place = xp_recv.at[minus(t, kt, n_t) % parts, minus(s, k, n_seq)]
        return remote(place, place, xp_ss.at[kt, k], xp_rs.at[kt, k],
                      {"seq": plus(s, k, n_seq), "tensor": plus(t, kt, n_t)})

    for kt in range(parts):
        @pl.loop(0 if kt else 1, n_seq)
        def _(k):
            xp_copy(kt, k).start()

    xp_recv[part, s] = xp_send[0, s]
    turned[...] = scol[...].reshape(image_total, width).T

    @over_seq
    def _(k):
        landed(vp_recv, vp_ss, vp_rs, k).wait_recv()

    vg_all[t, s] = vp_recv[...].astype(F32).sum(0).astype(BF16)

    def vg_copy(m):
        return remote(
            vg_all.at[t, s], vg_all.at[t, s], vg_ss.at[m], vg_rs.at[m],
            {"seq": plus(s, m // n_t, n_seq), "tensor": plus(t, m % n_t, n_t)},
        )

    def vg_goes(m):
        if parts > 1:
            return m > 0
        return jnp.logical_or(m % n_t == 0, lax.rem(s, n_t) == plus(t, m % n_t, n_t))

    @pl.loop(1, n_seq * n_t)
    def _(m):
        @pl.when(vg_goes(m))
        def _():
            vg_copy(m).start()

    for kt in range(parts):
        @pl.loop(0 if kt else 1, n_seq)
        def _(k):
            xp_arrived(kt, k).wait_recv()

    val_all[s] = xp_recv[...].astype(F32).sum((0, 1)).astype(BF16)

    def val_copy(k):
        return remote(val_all.at[s], val_all.at[s], val_ss.at[k], val_rs.at[k],
                      {"seq": plus(s, k, n_seq)})

    @over_seq
    def _(k):
        val_copy(k).start()

    @pl.loop(1, n_seq * n_t)
    def _(m):
        from_s = minus(s, m // n_t, n_seq)

        @pl.when(m > 0 if parts > 1 else jnp.logical_or(m % n_t == 0, lax.rem(from_s, n_t) == t))
        def _():
            source = vg_all.at[minus(t, m % n_t, n_t), from_s]
            remote(source, source, vg_ss.at[m], vg_rs.at[m],
                   {"seq": plus(s, m // n_t, n_seq), "tensor": plus(t, m % n_t, n_t)}).wait_recv()

    def grads_of(n):
        return jnp.concatenate(
            [vg_all[plus(t, kt, n_t)].reshape(image_total, HD) for kt in range(n)], axis=1
        )

    terms = dot(turned[...], grads_of(parts), 1, 0)
    for kt in range(parts):
        wg_send[kt] = terms[:, kt * HD : (kt + 1) * HD].astype(BF16)

    def wg_copy(kd, kt):
        return remote(wg_send.at[kt], wg_recv.at[d, rows_of(t)], wg_ss.at[kd, kt],
                      wg_rs.at[kd, kt],
                      {"dp": plus(d, kd, n_dp), "tensor": plus(t, kt, n_t)})

    wg_moves = [(kd, kt) for kd in reversed(range(n_dp)) for kt in range(parts) if kd + kt > 0]
    for kd, kt in wg_moves:
        wg_copy(kd, kt).start()
    wg_recv[d, rows_of(t)] = wg_send[0]

    if parts == 1:
        w_arrived()

    def image_term(c):
        rows = jnp.concatenate([vg_all[c, j * n_t + t] for j in range(per_t)], axis=0)
        return dot(rows, w_all[c], 1, 1).astype(BF16).astype(F32)

    if parts > 1:
        total = dot(grads_of(n_t), weight_part(n_t), 1, 1)
    else:
        total = image_term(0)
        for c in range(1, n_t):
            total = total + image_term(c)
    blocks = ig_send.shape[0]
    ig_send[...] = total.astype(BF16).reshape(blocks, img_dev, width)

    to_t = s // per_t
    slot = cols_of(lax.rem(s, per_t))
    place_in = lax.rem(s, per_t) * parts + part

    def row_block(j):
        return j if parts > 1 else j * n_t + t

    def ig_copy(j):
        return remote(ig_send.at[j], ig_recv.at[:, slot], ig_ss.at[j], ig_rs.at[place_in],
                      {"seq": row_block(j), "tensor": to_t})

    def ig_stays(j):
        return jnp.logical_and(row_block(j) == s, to_t == t)

    for j in range(blocks):
        @pl.when(jnp.logical_not(ig_stays(j)))
        def _():
            ig_copy(j).start()

        @pl.when(ig_stays(j))
        def _():
            ig_recv[:, slot] = ig_send[j]

    @over_seq
    def _(k):
        landed(val_all, val_ss, val_rs, k).wait_recv()

    kp_acc[...] = jnp.zeros_like(kp_acc)

    @pl.loop(0, heads, unroll=heads)
    def _(h):
        cols = pl.ds(pl.multiple_of(h * HD, HD), HD)
        slopes = dot(val_all[...].reshape(image_total, HD), og_ref[0, :, cols], 1, 1)
        p = probs[h]
        delta = (p * slopes).sum(0, keepdims=True)
        ds = (p * (slopes - delta) * inv_root).astype(BF16)
        kp_acc[...] += dot(ds, q_ref[0, :, cols], 1, 0)
        keys = keys_all[...].reshape(image_total, HD)
        qg_ref[0, :, cols] = dot(ds, keys, 0, 0).astype(BF16)

    qg_out = pltpu.make_async_copy(qg_ref, qg_hbm, out_sem.at[0])
    qg_out.start()
    kp_send[...] = kp_acc[...].astype(BF16).reshape(n_seq, img_dev, HD)

    @over_seq
    def _(k):
        scatter_copy(kp_send, kp_recv, kp_ss, kp_rs, k).start()

    kp_recv[s] = kp_send[s]

    for kd, kt in wg_moves:
        place = wg_recv.at[minus(d, kd, n_dp), rows_of(minus(t, kt, n_t))]
        remote(place, place, wg_ss.at[kd, kt], wg_rs.at[kd, kt],
               {"dp": plus(d, kd, n_dp), "tensor": plus(t, kt, n_t)}).wait_recv()
    wg_ref[...] = wg_recv[...].astype(F32).sum(0).astype(BF16)
    wg_out = pltpu.make_async_copy(wg_ref, wg_hbm, out_sem.at[1])
    wg_out.start()

    for j in range(per_t * parts):
        from_s = t * per_t + j // parts
        from_t = j % parts if parts > 1 else lax.rem(s, n_t)

        @pl.when(jnp.logical_not(jnp.logical_and(from_s == s, from_t == t)))
        def _():
            place = ig_recv.at[:, pl.ds(j * width, width)]
            remote(ig_send.at[0], place, ig_ss.at[j], ig_rs.at[j],
                   {"seq": from_s, "tensor": from_t}).wait_recv()

    ig_out = pltpu.make_async_copy(ig_recv, ig_hbm.at[0], out_sem.at[2])
    ig_out.start()

    @over_seq
    def _(k):
        landed(kp_recv, kp_ss, kp_rs, k).wait_recv()

    kg_ref[0] = kp_recv[...].astype(F32).sum(0).astype(BF16)

    kg_out = pltpu.make_async_copy(kg_ref, kg_hbm, out_sem.at[3])
    kg_out.start()

    for kt in range(parts):
        @pl.loop(0 if kt else 1, n_seq)
        def _(k):
            xp_copy(kt, k).wait_send()

    @over_seq
    def _(k):
        keys_copy(k).wait_send()
        st_copy(k).wait_send()
        scatter_copy(vp_send, vp_recv, vp_ss, vp_rs, k).wait_send()
        val_copy(k).wait_send()
        scatter_copy(kp_send, kp_recv, kp_ss, kp_rs, k).wait_send()

    @pl.loop(1, n_seq * n_t)
    def _(m):
        @pl.when(vg_goes(m))
        def _():
            vg_copy(m).wait_send()

    for k in range(1, n_t):
        w_copy(k).wait_send()
    for kd, kt in wg_moves:
        wg_copy(kd, kt).wait_send()
    for j in range(blocks):
        @pl.when(jnp.logical_not(ig_stays(j)))
        def _():
            ig_copy(j).wait_send()
    for copy in (qg_out, wg_out, ig_out, kg_out):
        copy.wait()


def write_out(*refs):
    sems = refs[12]
    ins = [pltpu.make_async_copy(refs[i], refs[8 + i], sems.at[0, i]) for i in range(4)]
    outs = [pltpu.make_async_copy(refs[8 + i], refs[4 + i], sems.at[1, i]) for i in range(4)]
    for copy in ins:
        copy.start()
    for arrived, leaves in zip(ins, outs):
        arrived.wait()
        leaves.start()
    for copy in outs:
        copy.wait()


def on_device(n_dp, n_seq, n_t, queries, image_keys, image_states, value_weight, out_grad):
    img_dev = image_keys.shape[1]
    image_total = n_seq * img_dev
    text_rows = queries.shape[1]
    heads = queries.shape[2] // HD
    d_model = image_states.shape[2]
    d_seq = value_weight.shape[0]
    d_t = d_model // n_t
    per_t = n_seq // n_t
    parts = n_t if d_seq % (n_t * 128) == 0 else 1
    width = d_seq // parts
    vmem = pltpu.VMEM
    rows = (n_seq, img_dev, HD)
    scratch = [
        vmem(queries.shape, BF16),
        vmem(image_keys.shape, BF16),
        vmem(value_weight.shape, BF16),
        vmem((1, img_dev, d_t), BF16),
        vmem(queries.shape, BF16),
        vmem(out_grad.shape, BF16),
        vmem(rows, BF16),
        vmem((n_seq, img_dev, width), BF16),
        vmem((width, image_total), BF16),
        vmem((n_t, d_seq, HD), BF16),
        vmem((heads, image_total, text_rows), F32),
        vmem((image_total, HD), F32),
        vmem(rows, BF16),
        vmem(rows, BF16),
        vmem((parts,) + rows, XP),
        vmem((parts,) + rows, XP),
        vmem((n_t,) + rows, BF16),
        vmem(rows, BF16),
        vmem((image_total, HD), F32),
        vmem(rows, BF16),
        vmem(rows, BF16),
        vmem((parts, width, HD), BF16),
        vmem((n_dp, d_seq, HD), BF16),
        vmem((per_t * parts, img_dev, width), BF16),
        vmem((img_dev, d_t), BF16),
    ]
    counts = [
        (n_seq,), (n_seq,), (n_t,), (n_seq,), (parts, n_seq), (n_seq * n_t,), (n_seq,), (n_seq,),
        (n_dp, parts), (per_t * parts,),
    ]
    sems = [pltpu.SemaphoreType.DMA((4,))] + [pltpu.SemaphoreType.DMA((5,))] + [pltpu.SemaphoreType.DMA(c) for c in counts for _ in range(2)]
    spec = pl.BlockSpec(memory_space=pltpu.VMEM)
    grads = pl.pallas_call(
        functools.partial(kernel, n_dp, n_seq, n_t),
        out_shape=(
            jax.ShapeDtypeStruct(queries.shape, BF16),
            jax.ShapeDtypeStruct(image_keys.shape, BF16),
            jax.ShapeDtypeStruct(value_weight.shape, BF16),
            jax.ShapeDtypeStruct((1, img_dev, d_t), BF16),
        ),
        in_specs=[pl.BlockSpec(memory_space=pltpu.HBM)] * 5,
        out_specs=(pl.BlockSpec(memory_space=pltpu.HBM),) * 4,
        scratch_shapes=scratch + sems,
        compiler_params=pltpu.CompilerParams(
            collective_id=0, has_side_effects=True, vmem_limit_bytes=63 * 1024 * 1024
        ),
    )(queries, image_keys, image_states, value_weight, out_grad)
    return pl.pallas_call(
        write_out,
        out_shape=tuple(jax.ShapeDtypeStruct(g.shape, g.dtype) for g in grads),
        in_specs=[pl.BlockSpec(memory_space=pltpu.HBM)] * 4,
        out_specs=(pl.BlockSpec(memory_space=pltpu.HBM),) * 4,
        scratch_shapes=[vmem(g.shape, g.dtype) for g in grads] + [pltpu.SemaphoreType.DMA((2, 4))],
        compiler_params=pltpu.CompilerParams(vmem_limit_bytes=63 * 1024 * 1024),
    )(*grads)


def solution(mesh):
    in_specs = (
        P("dp", "seq", "tensor"),
        P("dp", "seq", "tensor"),
        P("dp", "seq", None),
        P("seq", "tensor"),
        P("dp", "seq", "tensor"),
    )
    out_specs = (
        P("dp", "seq", "tensor"),
        P("dp", "seq", "tensor"),
        P("seq", "tensor"),
        P("dp", "seq", "tensor"),
    )
    sizes = (mesh.shape["dp"], mesh.shape["seq"], mesh.shape["tensor"])
    return jax.shard_map(
        functools.partial(on_device, *sizes),
        mesh=mesh, in_specs=in_specs, out_specs=out_specs, check_vma=False,
    )
```
